512 devices in a mesh: section: 8 (over z_hi, x), dp: 64 (over y, z_lo, core).
Axes of the slice: x: 4, y: 8, z: 8 (z_hi: 2, z_lo: 4; z = z_hi * 4 + z_lo), core: 2. Of those that a mesh axis runs over, the one named last changes fastest.
Arguments:
- x_down: bfloat16 [8, 8192, 1024], P('section', 'dp'), may hold values from -16 to 16
- x_up: bfloat16 [8, 8192, 1024], P('section', 'dp'), may hold values from -16 to 16
- weights: bfloat16 [8, 2, 1024, 1024], P('section', None, 'dp'), as said below
- cot_down: bfloat16 [8192, 1024], P('dp'), may hold values from -6 to 6
- cot_up: bfloat16 [8192, 1024], P('dp'), may hold values from -6 to 6
Outputs:
- grad_down: bfloat16 [8, 8192, 1024], P('section', 'dp')
- grad_up: bfloat16 [8, 8192, 1024], P('section', 'dp')
- grad_w: float32 [8, 1024, 1024], P('section', 'dp')
The draws below stay inside these ranges and needn't reach their ends.
Inputs may be any that keep to these rules, and one draw needn't show every extreme that they name: weights[j, 1] is the same matrix as weights[7 - j, 0].
All inputs are finite; a program needn't handle non-finite values.
Results may differ from the reference program's by a relative error of at most 0.009.
Values may be sent and summed in bfloat16 or wider, within the bound.
A program may use at most 64 MiB of HBM per device.

```python
import math
import jax
import jax.numpy as jnp
from jax import lax

D = 1024
TOKENS = 8192
N_SECTION = 8


def draw_weights(key, part):
    key = jax.random.fold_in(key, 11)
    base = jax.random.normal(key, (N_SECTION, D, D), jnp.float32)
    base = base * (1.0 / math.sqrt(D))
    return jnp.stack([base, base[::-1]], axis=1).astype(jnp.bfloat16)


def strengthened(result, own_key, source, target, parts, factor):
    owner, partner = [(jnp.arange(result.shape[axis_at]) // (result.shape[axis_at] // parts)).reshape([-1 if axis == axis_at else 1 for axis in range(result.ndim)]) for axis_at in (source, target)]
    chosen = jax.random.permutation(own_key, parts)[partner]
    strong = (owner == chosen) | (owner == (partner + parts // 2) % parts)
    return jnp.where(strong, factor * result, result)


def block_levels(rng, shape, shards, smallest, high):
    level, own = 1.0, jax.random.fold_in(rng, 6)
    for axis_at, shards_of in shards:
        heights = jnp.exp(jax.random.uniform(jax.random.fold_in(own, axis_at), (shards_of,), jnp.float32, smallest / len(shards), high / len(shards)))
        level = level * jnp.repeat(heights, shape[axis_at] // shards_of).reshape([-1 if axis == axis_at else 1 for axis in range(len(shape))])
    return level


def noise(own_key, dims, scale, most, shards=(), held_as=jnp.bfloat16):
    result = scale * jax.random.normal(own_key, dims, jnp.float32)
    if shards:
        result = result * block_levels(own_key, dims, shards, -0.22, 0.18)
    return jnp.clip(result, -most, most).astype(held_as)


def heavy_noise(stream_key, dims, deviation, reach, pieces, heavy, held_as=jnp.bfloat16):
    result = deviation * jax.random.normal(stream_key, dims, jnp.float32)
    if pieces:
        result = result * block_levels(stream_key, dims, pieces, -0.22, 0.18)
    return jnp.clip(strengthened(result, jax.random.fold_in(stream_key, 3), *heavy), -reach, reach).astype(held_as)


def setup_inputs(seed: int = 0) -> dict:
    splits = jax.random.split(jax.random.key(seed), 6)
    return {
        "x_down": heavy_noise(splits[0], (N_SECTION, TOKENS, D), 1.0, 16.0, ((0, 8), (1, 64)), (1, 2, 64, 4.0)),
        "x_up": heavy_noise(splits[1], (N_SECTION, TOKENS, D), 1.0, 16.0, ((0, 8), (1, 64)), (1, 2, 64, 4.0)),
        "weights": draw_weights(jax.random.fold_in(splits[5], 71), 0),
        "cot_down": noise(splits[3], (TOKENS, D), 1.0, 6.0, ((0, 64),)),
        "cot_up": noise(splits[4], (TOKENS, D), 1.0, 6.0, ((0, 64),)),
    }


def gelu_slope(pre):
    cdf = 0.5 * (1.0 + lax.erf(pre * (1.0 / math.sqrt(2.0))))
    return cdf + pre * jnp.exp(-0.5 * pre * pre) * (1.0 / math.sqrt(2.0 * math.pi))

def section_back(inputs, weight, upstream):
    pre = jnp.dot(inputs, weight, preferred_element_type=jnp.float32)
    delta = (gelu_slope(pre) * upstream.astype(jnp.float32)).astype(jnp.bfloat16)
    carried = lax.dot_general(delta, weight, (((1,), (1,)), ((), ())), preferred_element_type=jnp.float32)
    back = (upstream.astype(jnp.float32) + carried).astype(jnp.bfloat16)
    return (delta, back)

def reference(x_down, x_up, weights, cot_down, cot_up):
    count = N_SECTION
    scale = 1.0 / math.sqrt(2.0 * TOKENS)
    down_grads = [None] * count
    down_deltas = [None] * count
    upward = cot_down
    for section in reversed(range(count)):
        delta, upward = section_back(x_down[section], weights[section, 0], upward)
        down_grads[section] = upward
        down_deltas[section] = delta
    up_grads = [None] * count
    up_deltas = [None] * count
    upward = cot_up
    for section in reversed(range(count)):
        holder = count - 1 - section
        delta, upward = section_back(x_up[holder], weights[holder, 1], upward)
        up_grads[holder] = upward
        up_deltas[holder] = delta
    weight_grads = []
    for section in range(count):
        holder = count - 1 - section
        first = lax.dot_general(x_down[section], down_deltas[section], (((0,), (0,)), ((), ())), preferred_element_type=jnp.float32)
        second = lax.dot_general(x_up[holder], up_deltas[holder], (((0,), (0,)), ((), ())), preferred_element_type=jnp.float32)
        weight_grads.append((first + second) * scale)
    return (jnp.stack(down_grads), jnp.stack(up_grads), jnp.stack(weight_grads))
```

```python
import functools
import math

import jax
import jax.numpy as jnp
from jax import lax
from jax.experimental import pallas as pl
from jax.experimental.pallas import tpu as pltpu
from jax.sharding import PartitionSpec as P

Y, Z, C = 8, 4, 2
SECTIONS = 8
D = 1024
H = D // 2
ROWS = 128
SHARD = 16
MICRO = 4
STEP = ROWS // MICRO
HALF = ((0, 1), (2, 3))
MESH = pl.DeviceIdType.MESH
F32, BF16 = jnp.float32, jnp.bfloat16


def gelu_slope(pre):
    cdf = 0.5 * (1.0 + lax.erf(pre * (1.0 / math.sqrt(2.0))))
    return cdf + pre * jnp.exp(-0.5 * pre * pre) * (1.0 / math.sqrt(2.0 * math.pi))


def kernel(
    x_down, x_up, weights, cot_down, cot_up, grad_down, grad_up, grad_w,
    w, x, g_in, g_out, slope, delta, part, y_in, y_own, z_out, z_in, total, far_out, far_in, gw,
    load_sem, out_sem,
    agz_s, agz_r, agy_s, agy_r, agc_s, agc_r,
    xc_s, xc_r, ch_s, ch_r, dc_s, dc_r,
    rsy_s, rsy_r, rsz_s, rsz_r, far_s, far_r,
):
    s = lax.axis_index("section")
    me = lax.axis_index("dp")
    y, z, c = me // (Z * C), (me // C) % Z, me % C
    hi = s // (SECTIONS // 2)
    p = s + hi * (SECTIONS - 1 - 2 * s)
    ahead = 1 - 2 * hi

    def dev(ss, yy, zz, cc):
        return (ss, (yy * Z + zz) * C + cc)

    def send(src, dst, send_sem, recv_sem, to):
        return pltpu.make_async_remote_copy(
            src_ref=src, dst_ref=dst, send_sem=send_sem, recv_sem=recv_sem,
            device_id=to, device_id_type=MESH,
        )

    sibling = dev(s, y, z, 1 - c)

    def y_at(step):
        return (y + step + 2 * Y) % Y

    def z_at(step):
        return (z + step + 2 * Z) % Z

    def loads():
        @pl.when(hi == 1)
        def _():
            pltpu.make_async_copy(x_down, x.at[0, c], load_sem.at[0]).start()
            pltpu.make_async_copy(x_up, x.at[1, c], load_sem.at[1]).start()

        @pl.when(hi == 0)
        def _():
            pltpu.make_async_copy(x_up, x.at[0, c], load_sem.at[0]).start()
            pltpu.make_async_copy(x_down, x.at[1, c], load_sem.at[1]).start()

        for i in range(MICRO):
            rows = pl.ds(i * STEP, STEP)

            @pl.when(s == SECTIONS - 1)
            def _():
                pltpu.make_async_copy(cot_down.at[rows], g_in.at[0, rows], ch_r.at[0, i]).start()

            @pl.when(s == 0)
            def _():
                pltpu.make_async_copy(cot_up.at[rows], g_in.at[0, rows], ch_r.at[0, i]).start()

    def own_weight(r):
        index = 1 - hi if r == 0 else hi
        return pltpu.make_async_copy(weights.at[index], w.at[r, y, z, c], load_sem.at[2 + r])

    def agz(r, k):
        block = w.at[r, y, z, c]
        return send(block, block, agz_s.at[r, k - 1], agz_r.at[r, k - 1], dev(s, y, z_at(k), c))

    def agz_in(r, k):
        block = w.at[r, y, z_at(-k), c]
        return send(block, block, agz_s.at[r, k - 1], agz_r.at[r, k - 1], dev(s, y, z_at(k), c))

    def agy(r, d, t, j, arriving=False):
        sign = 1 - 2 * d
        block = w.at[r, y_at(-sign * (t + 1 if arriving else t)), z_at(-j), c]
        to = dev(s, y_at(sign), z, c)
        return send(block, block, agy_s.at[r, d, t, j], agy_r.at[r, d, t, j], to)

    def agc(r, k, arriving=False):
        origin = (1, 2, 3, -1, -2, -3, 0, 4)[k]
        block = w.at[r, y_at(-origin), :, 1 - c if arriving else c]
        return send(block, block, agc_s.at[r, k], agc_r.at[r, k], sibling)

    def ag_z_start(r):
        own_weight(r).wait()
        for k in range(1, Z):
            agz(r, k).start()

    def ag_y_start(r):
        for j in range(Z):
            if j:
                agz_in(r, j).wait_recv()
            for d in range(2):
                agy(r, d, 0, j).start()
        agc(r, 6).start()

    def ag_y_forward(r):
        for t in range(1, 4):
            for j in range(Z):
                for d in range(2):
                    agy(r, d, t - 1, j, True).wait_recv()
                    if t < 3 or j in HALF[d]:
                        agy(r, d, t, j).start()
            for d in range(2):
                agc(r, d * 3 + t - 1).start()
        for d in range(2):
            for j in HALF[d]:
                agy(r, d, 3, j, True).wait_recv()
        agc(r, 7).start()

    def ag_sends_done(r):
        for k in range(1, Z):
            agz(r, k).wait_send()
        for d in range(2):
            for t in range(4):
                for j in range(Z):
                    if t < 3 or j in HALF[d]:
                        agy(r, d, t, j).wait_send()
        for k in range(8):
            agc(r, k).wait_send()

    def weight(r):
        return w[r].reshape(D, D)

    def prepare(r):
        for k in range(8):
            agc(r, k, True).wait_recv()
        pre = jnp.dot(x[r, c], weight(r), preferred_element_type=F32)
        slope[r] = gelu_slope(pre)

    def dc(r, i, arriving=False):
        block = delta.at[r, 1 - c, c, pl.ds(i * STEP, STEP)] if arriving else delta.at[r, c, 1 - c, pl.ds(i * STEP, STEP)]
        return send(block, block, dc_s.at[r, i], dc_r.at[r, i], sibling)

    def hop(r, i):
        rows = pl.ds(i * STEP, STEP)
        if r == 0:
            slot, to = p // 3, dev(s + ahead, y, z, c)
        else:
            slot, to = 1, dev(s - ahead, y, z, c)
        return send(g_out.at[r, rows], g_in.at[slot, rows], ch_s.at[r, i], ch_r.at[slot, i], to)

    def hop_in(r, i):
        rows = pl.ds(i * STEP, STEP)
        return pltpu.make_async_copy(g_out.at[r, rows], g_in.at[r, rows], ch_r.at[r, i])

    def chain(r):
        for i in range(MICRO):
            rows = pl.ds(i * STEP, STEP)
            hop_in(r, i).wait()
            g = g_in[r, rows, :].astype(F32)
            d = (slope[r, rows, :] * g).astype(BF16)
            delta[r, c, 0, rows, :] = d[:, :H]
            delta[r, c, 1, rows, :] = d[:, H:]
            dc(r, i).start()
            carried = lax.dot_general(
                d, weight(r), (((1,), (1,)), ((), ())), preferred_element_type=F32
            )
            g_out[r, rows, :] = (g + carried).astype(BF16)
            if r == 0:
                hop(r, i).start()
            else:
                pl.when(p > 0)(hop(r, i).start)

    def store_grads(r, wait=False):
        if wait:
            pltpu.make_async_copy(g_out.at[r], grad_down, out_sem.at[r]).wait()
            return
        for value in range(2):
            out = grad_down if value != r else grad_up
            pl.when(hi == value)(pltpu.make_async_copy(g_out.at[r], out, out_sem.at[r]).start)

    def xc(r, arriving=False):
        block = x.at[r, 1 - c if arriving else c]
        return send(block, block, xc_s.at[r], xc_r.at[r], sibling)

    def rsy(r, d, t, q, arriving=False):
        sign = 1 - 2 * d
        if t == 0 or (t == 1 and q not in HALF[d]):
            src = y_own.at[r, d, q]
        else:
            src = y_in.at[r, d, t - 1, q]
        dst = y_in.at[r, d, t, q]
        to = dev(s, y_at(sign), z, c)
        return send(src, dst, rsy_s.at[r, d, t, q], rsy_r.at[r, d, t, q], to)

    def rsz(r, k, e, arriving=False):
        src = z_out.at[r, z_at(k), (c + e) % C]
        dst = z_in.at[r, z_at(-k), (c + e) % C] if arriving else z_in.at[r, z, c]
        return send(src, dst, rsz_s.at[r, k, e], rsz_r.at[r, k, e], dev(s, y, z_at(k), (c + e) % C))

    def far():
        return send(far_out, far_in, far_s, far_r, dev(SECTIONS - 1 - s, y, z, c))

    def reduce(r):
        xc(r, True).wait_recv()
        for i in range(MICRO):
            dc(r, i, True).wait_recv()
        xs = x[r].reshape(C * ROWS, D)
        ds = jnp.concatenate([delta[r, 0, c], delta[r, 1, c]], axis=0)
        product = lax.dot_general(xs, ds, (((0,), (0,)), ((), ())), preferred_element_type=F32)
        part[...] = product.reshape(Y, Z, C * SHARD, H)
        for t in range(4):
            for arrived in (False, True):
                for q in range(Z):
                    for d in range(2):
                        sign = 1 - 2 * d
                        mine = part.at[y_at(sign * (4 - t)), q]
                        first = t == 0 or (t == 1 and q not in HALF[d])
                        if first == arrived or (t == 0 and q not in HALF[d]):
                            continue
                        if first:
                            y_own[r, d, q] = mine[...].astype(BF16)
                        else:
                            rsy(r, d, t - 1, q).wait_recv()
                            y_in[r, d, t - 1, q] = (y_in[r, d, t - 1, q].astype(F32) + mine[...]).astype(BF16)
                        rsy(r, d, t, q).start()
        for q in range(Z):
            for d in range(2):
                rsy(r, d, 3, q).wait_recv()
            total_q = part[y, q] + y_in[r, 0, 3, q].astype(F32) + y_in[r, 1, 3, q].astype(F32)
            z_out[r, q] = total_q.astype(BF16).reshape(C, SHARD, H)
        for k in range(Z):
            for e in range(C):
                if k or e:
                    rsz(r, k, e).start()
        z_in[r, z, c] = z_out[r, z, c]
        for k in range(Z):
            for e in range(C):
                if k or e:
                    rsz(r, k, e, True).wait_recv()
        for h in range(C):
            total[r, :, h * H : (h + 1) * H] = sum(z_in[r, q, h].astype(F32) for q in range(Z))

        @pl.when(hi == r)
        def _():
            far_out[...] = total[r].astype(BF16)
            far().start()

    def reduce_sends_done(r):
        for i in range(MICRO):
            dc(r, i).wait_send()
        for d in range(2):
            for t in range(4):
                for q in range(Z):
                    if t > 0 or q in HALF[d]:
                        rsy(r, d, t, q).wait_send()
        for k in range(Z):
            for e in range(C):
                if k or e:
                    rsz(r, k, e).wait_send()

    for r in range(2):
        own_weight(r).start()
    loads()
    barrier = pltpu.get_barrier_semaphore()
    greeted = [sibling, dev(s, y_at(1), z, c), dev(s, y_at(-1), z, c)]
    greeted += [dev(s, y, z_at(k), cc) for k in range(1, Z) for cc in (c, 1 - c)]
    greeted += [
        dev((s + 1) % SECTIONS, y, z, c),
        dev((s + SECTIONS - 1) % SECTIONS, y, z, c),
        dev(SECTIONS - 1 - s, y, z, c),
    ]
    for device in greeted:
        pl.semaphore_signal(barrier, inc=1, device_id=device, device_id_type=MESH)
    pl.semaphore_wait(barrier, len(greeted))

    ag_z_start(0)
    ag_z_start(1)
    ag_y_start(0)
    for r in range(2):
        pltpu.make_async_copy(x_down, x.at[r, c], load_sem.at[r]).wait()
        xc(r).start()
    ag_y_forward(0)
    ag_y_start(1)
    prepare(0)

    def second_weight():
        ag_y_forward(1)
        prepare(1)

    pl.when(p >= 2)(second_weight)
    chain(0)
    store_grads(0)

    @pl.when(p < 2)
    def _():
        second_weight()
        reduce(0)

    chain(1)
    store_grads(1)

    @pl.when(p >= 2)
    def _():
        reduce(0)

    reduce(1)

    far().wait_recv()
    gw[...] = (total[1 - hi] + far_in[...].astype(F32)) * (1.0 / math.sqrt(2.0 * Y * Z * C * ROWS))
    copy = pltpu.make_async_copy(gw, grad_w, out_sem.at[2])
    copy.start()
    for r in range(2):
        ag_sends_done(r)
        xc(r).wait_send()
        reduce_sends_done(r)
        for i in range(MICRO):
            if r == 0:
                hop(r, i).wait_send()
            else:
                pl.when(p > 0)(hop(r, i).wait_send)
        store_grads(r, True)
    far().wait_send()
    copy.wait()


def per_device(x_down, x_up, weights, cot_down, cot_up):
    dma = pltpu.SemaphoreType.DMA
    anywhere = pl.BlockSpec(memory_space=pl.ANY)
    grad_down, grad_up, grad_w = pl.pallas_call(
        kernel,
        out_shape=(
            jax.ShapeDtypeStruct((ROWS, D), BF16),
            jax.ShapeDtypeStruct((ROWS, D), BF16),
            jax.ShapeDtypeStruct((SHARD, D), F32),
        ),
        in_specs=[anywhere] * 5,
        out_specs=(anywhere,) * 3,
        scratch_shapes=[
            pltpu.VMEM((2, Y, Z, C, SHARD, D), BF16),
            pltpu.VMEM((2, C, ROWS, D), BF16),
            pltpu.VMEM((2, ROWS, D), BF16),
            pltpu.VMEM((2, ROWS, D), BF16),
            pltpu.VMEM((2, ROWS, D), F32),
            pltpu.VMEM((2, C, 2, ROWS, H), BF16),
            pltpu.VMEM((Y, Z, C * SHARD, H), F32),
            pltpu.VMEM((2, 2, 4, Z, C * SHARD, H), BF16),
            pltpu.VMEM((2, 2, Z, C * SHARD, H), BF16),
            pltpu.VMEM((2, Z, C, SHARD, H), BF16),
            pltpu.VMEM((2, Z, C, SHARD, H), BF16),
            pltpu.VMEM((2, SHARD, D), F32),
            pltpu.VMEM((SHARD, D), BF16),
            pltpu.VMEM((SHARD, D), BF16),
            pltpu.VMEM((SHARD, D), F32),
            dma((4,)), dma((3,)),
            dma((2, 3)), dma((2, 3)), dma((2, 2, 4, Z)), dma((2, 2, 4, Z)), dma((2, 8)), dma((2, 8)),
            dma((2,)), dma((2,)), dma((2, MICRO)), dma((2, MICRO)), dma((2, MICRO)), dma((2, MICRO)),
            dma((2, 2, 4, Z)), dma((2, 2, 4, Z)), dma((2, Z, C)), dma((2, Z, C)), dma, dma,
        ],
        compiler_params=pltpu.CompilerParams(
            collective_id=0, has_side_effects=True, vmem_limit_bytes=40 << 20
        ),
        cost_estimate=pl.CostEstimate(
            flops=3 * 2 * 2 * ROWS * D * D, bytes_accessed=4 << 20, transcendentals=4 * ROWS * D
        ),
    )(x_down[0], x_up[0], weights[0], cot_down, cot_up)
    return grad_down[None], grad_up[None], grad_w[None]


def solution(mesh):
    in_specs = (
        P("section", "dp", None),
        P("section", "dp", None),
        P("section", None, "dp", None),
        P("dp", None),
        P("dp", None),
    )
    out_specs = (P("section", "dp", None), P("section", "dp", None), P("section", "dp", None))
    return jax.shard_map(
        per_device, mesh=mesh, in_specs=in_specs, out_specs=out_specs, check_vma=False
    )
```
